256 devices in a mesh: section: 8 (over x, y_lo), dp: 32 (over y_hi, z, core).
Axes of the slice: x: 4, y: 4 (y_hi: 2, y_lo: 2; y = y_hi * 2 + y_lo), z: 8, core: 2. Of those that a mesh axis runs over, the one named last changes fastest.
Arguments:
- normed_input: bfloat16 [8, 4096, 2048], P('section', 'dp'), may hold values from -6 to 6
- output_grad: bfloat16 [8, 4096, 2048], P('section', 'dp'), may hold values from -6 to 6
- expert_ids: int32 [8, 4096, 6], P('section', 'dp'), may hold values from 0 to 31, all different within a row; in each aligned block of 128 rows (0 to 127, 128 to 255, ..., all dimensions but the last counted through in order) at most 32 rows name the same one
- router_weight: float32 [8, 2048, 32], P('section'), may hold values from -0.125 to 0.125
- gate_up: bfloat16 [8, 32, 2048, 1408], P('section', 'dp'), may hold values from -0.125 to 0.125
- down_weight: bfloat16 [8, 32, 704, 2048], P('section', 'dp'), may hold values from -0.21875 to 0.21875
- saved_preact: bfloat16 [8, 32, 1024, 1408], P('section', 'dp'), may hold values from -8 to 8
- latent_input: bfloat16 [8, 4096, 2048], P('section', 'dp'), may hold values from -6 to 6
- latent_grad: bfloat16 [8, 4096, 512], P('section', 'dp'), may hold values from -6 to 6
- momentum: float32 [8, 2048, 512], P('section', 'dp'), may hold values from -200 to 200
Outputs:
- input_grad: bfloat16 [8, 4096, 2048], P('section', 'dp')
- momentum_next: float32 [8, 2048, 512], P('section', 'dp')
- muon_update: bfloat16 [8, 2048, 512], P('section', 'dp')
The draws below stay inside these ranges and needn't reach their ends.
Inputs may be any that keep to these rules, and one draw needn't show every extreme that they name: `expert_ids`: each token's 6 ids are distinct. Among the tokens of one device no expert is named more than 32 times, a bound that some block reaches.
All inputs are finite; a program needn't handle non-finite values.
Results may differ from the reference program's by a relative error of at most 0.027.
Values may be sent and summed in bfloat16 or wider, within the bound.
No kernel may reach another device: no remote copies, remote signals or barrier semaphores. Data moves between devices by JAX's collectives and lax.ppermute only.
A program may use at most 128 MiB of HBM per device.

```python
import math
import jax
import jax.numpy as jnp
import numpy as np
from jax import lax

D = 2048
FFW = 704
KVA = 512
TOP = 6
NS_ITERS = 2
TOK_DEV = 128
SECTIONS = 8
EXPERTS = 32
TOKENS = 4096
CAP = 32
N_DP = 32


def draw_momentum(key, part):
    key = jax.random.fold_in(key, 7)
    base_key, row_key, column_key = jax.random.split(key, 3)
    row_scale = jnp.exp(jax.random.uniform(row_key, (SECTIONS, D, 1), jnp.float32, 0.0, math.log(10.0)))
    column_scale = jnp.exp(jax.random.uniform(column_key, (SECTIONS, 1, KVA), jnp.float32, 0.0, math.log(10.0)))
    base = jnp.clip(jax.random.normal(base_key, (SECTIONS, D, KVA), jnp.float32), -4.0, 4.0)
    return jnp.clip(0.5 * base * row_scale * column_scale, -200.0, 200.0)


def spiked(result, own_key, source, target, blocks, factor):
    owner, partner = [(jnp.arange(result.shape[dim]) // (result.shape[dim] // blocks)).reshape([-1 if axis == dim else 1 for axis in range(result.ndim)]) for dim in (source, target)]
    chosen = jax.random.permutation(own_key, blocks)[partner]
    strong = (owner == chosen) | (owner == (partner + blocks // 2) % blocks)
    return jnp.where(strong, factor * result, result)


def block_scale(stream_key, shape, pieces, low, high):
    loudness = 1.0
    for dim, shards_of in pieces:
        draws = jax.random.uniform(jax.random.fold_in(jax.random.fold_in(stream_key, 6), dim), (shards_of,), jnp.float32, low / len(pieces), high / len(pieces))
        loudness = loudness * jnp.repeat(jnp.exp(draws), shape[dim] // shards_of).reshape((-1,) + (1,) * (len(shape) - 1 - dim))
    return loudness


def shared_out(rng, own, number, rows, number_of, top, limit, skew):
    sequence = jax.random.permutation(rng, number_of)
    heavy_load, common = portions_of(number_of, rows * top, limit, skew, True), portions_of(number_of, rows * top, limit, skew, False)
    places = jnp.arange(number_of)

    def named(lengths, turn):
        used = int((lengths > 0).sum())
        fixed = max(1, used // 4)
        shifted = fixed + (places - fixed + turn * (used - fixed)) % max(1, number_of - fixed)
        return jnp.zeros((number_of,), jnp.int32).at[sequence[jnp.where(places < fixed, places, shifted)]].set(jnp.asarray(lengths, jnp.int32))

    lengths = jnp.where(number % 4 == 0, named(heavy_load, number // 4), named(common, number - number // 4 - 1))
    mixed = jax.random.permutation(jax.random.fold_in(own, 3), number_of)
    donor, receiver = mixed[0:number_of // 2 * 2:2], mixed[1:number_of // 2 * 2:2]
    slack = jnp.minimum(lengths[donor] - 1, limit - lengths[receiver]) // 2
    slack = jnp.where((donor == sequence[0]) | (receiver == sequence[0]) | (lengths[receiver] == 0), 0, jnp.maximum(slack, 0))
    shifted = jax.random.randint(jax.random.fold_in(own, 4), (number_of // 2,), 0, 1 << 20) % (slack + 1)
    lengths = lengths.at[donor].add(-shifted).at[receiver].add(shifted)
    labels = jnp.searchsorted(jnp.cumsum(lengths), jnp.arange(rows * top), side="right").astype(jnp.int32)
    listing = labels.reshape(top, rows).T
    listing = listing[jax.random.permutation(jax.random.fold_in(own, 1), rows)]
    turn = jax.random.randint(jax.random.fold_in(own, 2), (rows, 1), 0, top)
    return jnp.take_along_axis(listing, (jnp.arange(top)[None, :] + turn) % top, axis=1)


def portions_of(amount, total, limit, slope, full):
    weights = [(1 << 20) // math.isqrt(standing ** slope) + 1 for standing in range(1, amount + 1)]
    largest = limit if full else min(limit, max(-(-total // amount), total * weights[0] // sum(weights)))
    least = 1 if total - largest >= amount - 1 else 0
    counts, rest = [largest] + [least] * (amount - 1), total - largest - least * (amount - 1)
    while rest > 0:
        candidates = [i for i in range(1, amount) if counts[i] < largest] or [i for i in range(1, amount) if counts[i] < limit]
        pool, remaining = sum([weights[i] for i in candidates]), rest
        for i in candidates:
            extra = min(limit - counts[i], max(1, remaining * weights[i] // pool), rest)
            counts[i] = counts[i] + extra
            rest = rest - extra
    return np.array(counts)


def normal_values(key, extent, spread, reach, cuts=(), held_as=jnp.bfloat16):
    entries = spread * jax.random.normal(key, extent, jnp.float32)
    if cuts:
        entries = entries * block_scale(key, extent, cuts, -0.22, 0.18)
    return jnp.clip(entries, -reach, reach).astype(held_as)


def heavy_noise(stream_key, dims, scale, limit, pieces, heavy, kind=jnp.bfloat16):
    drawn = scale * jax.random.normal(stream_key, dims, jnp.float32)
    if pieces:
        drawn = drawn * block_scale(stream_key, dims, pieces, -0.22, 0.18)
    return jnp.clip(spiked(drawn, jax.random.fold_in(stream_key, 3), *heavy), -limit, limit).astype(kind)


def setup_inputs(seed: int = 0) -> dict:
    seeds = jax.random.split(jax.random.key(seed), 11)
    normed_input = normal_values(seeds[0], (SECTIONS, TOKENS, D), 1.0, 6.0, ((0, 8), (1, 32)))
    output_grad = normal_values(seeds[1], (SECTIONS, TOKENS, D), 1.0, 6.0, ((0, 8), (1, 32)))
    expert_ids_keys = jax.random.split(jax.random.fold_in(seeds[2], 1), SECTIONS * TOKENS // TOK_DEV)
    expert_ids_turns = jax.random.permutation(jax.random.fold_in(seeds[2], 3), SECTIONS * TOKENS // TOK_DEV)
    expert_ids = jax.vmap(lambda own, number: shared_out(jax.random.fold_in(seeds[2], 2), own, number, TOK_DEV, EXPERTS, TOP, CAP, 2))(expert_ids_keys, expert_ids_turns).reshape((SECTIONS, TOKENS, TOP))
    router_weight = normal_values(seeds[3], (SECTIONS, D, EXPERTS), D ** -0.5, 0.125, ((0, 8),), jnp.float32)
    gate_up = normal_values(seeds[4], (SECTIONS, EXPERTS, D, 2 * FFW), D ** -0.5, 0.125, ((0, 8), (1, 32)))
    down_weight = normal_values(seeds[5], (SECTIONS, EXPERTS, FFW, D), FFW ** -0.5, 0.21875, ((0, 8), (1, 32)))
    saved_preact = normal_values(seeds[6], (SECTIONS, EXPERTS, N_DP * CAP, 2 * FFW), 1.5, 8.0, ((0, 8), (1, 32)))
    latent_input = heavy_noise(seeds[7], (SECTIONS, TOKENS, D), 1.0, 6.0, ((0, 8), (1, 32)), (1, 2, 32, 2.75))
    latent_grad = normal_values(seeds[8], (SECTIONS, TOKENS, KVA), 1.0, 6.0, ((0, 8), (1, 32)))
    momentum = draw_momentum(jax.random.fold_in(seeds[10], 71), 0)
    return {"normed_input": normed_input, "output_grad": output_grad, "expert_ids": expert_ids, "router_weight": router_weight, "gate_up": gate_up, "down_weight": down_weight, "saved_preact": saved_preact, "latent_input": latent_input, "latent_grad": latent_grad, "momentum": momentum}


route_scale = 2.446
momentum_decay = 0.95
newton_a = 3.4445
newton_b = -4.775
newton_c = 2.0315
epsilon = 1e-07

def expert_backward(operands):
    received, gate_up_w, down_w, saved = operands
    width = down_w.shape[0]
    preact = saved.astype(jnp.float32)
    gate_pre = preact[:, :width]
    up_pre = preact[:, width:]
    gate_sigmoid = jax.nn.sigmoid(gate_pre)
    activated = gate_pre * gate_sigmoid
    hidden = activated * up_pre
    hidden_grad = lax.dot_general(received, down_w, (((1,), (1,)), ((), ())), preferred_element_type=jnp.float32)
    combine_grad = lax.optimization_barrier(jnp.sum(hidden_grad * hidden, axis=1)).astype(jnp.bfloat16)
    gate_grad = hidden_grad * up_pre * gate_sigmoid * (1.0 + gate_pre * (1.0 - gate_sigmoid))
    up_grad = hidden_grad * activated
    preact_grad = jnp.concatenate([gate_grad, up_grad], axis=1).astype(jnp.bfloat16)
    row_grad = lax.dot_general(preact_grad, gate_up_w, (((1,), (1,)), ((), ())), preferred_element_type=jnp.float32)
    return (row_grad.astype(jnp.bfloat16), combine_grad)

def router_backward(normed, chosen, router_w, token_rows, token_combine, experts):
    logits = jnp.dot(normed.astype(jnp.float32), router_w, precision=lax.Precision.HIGHEST, preferred_element_type=jnp.float32)
    scores = jax.nn.sigmoid(logits)
    choose = (chosen[:, :, None] == jnp.arange(experts, dtype=jnp.int32)[None, None, :]).astype(jnp.float32)
    picked = jnp.einsum('te,tke->tk', scores, choose, precision=lax.Precision.HIGHEST)
    denominator = lax.optimization_barrier(jnp.sum(picked, axis=1, keepdims=True))
    weights = route_scale * picked / denominator
    moe_part = lax.optimization_barrier(jnp.sum(weights[:, :, None] * token_rows, axis=1))
    select_grad = route_scale * (token_combine / denominator - lax.optimization_barrier(jnp.sum(token_combine * picked, axis=1, keepdims=True)) / (denominator * denominator))
    logit_part = select_grad * picked * (1.0 - picked)
    logit_grad = jnp.einsum('tk,tke->te', logit_part, choose, precision=lax.Precision.HIGHEST)
    router_part = lax.dot_general(logit_grad, router_w, (((1,), (1,)), ((), ())), precision=lax.Precision.HIGHEST, preferred_element_type=jnp.float32)
    return (moe_part + router_part).astype(jnp.bfloat16)

def section_backward(operands):
    normed, upstream, chosen, router_w, gate_up_w, down_w, saved = operands
    assigned = chosen.reshape(-1).astype(jnp.int32)
    count_all = assigned.shape[0]
    onehot = (assigned[:, None] == jnp.arange(EXPERTS, dtype=jnp.int32)[None, :]).astype(jnp.int32)
    per_source = onehot.reshape(N_DP, TOK_DEV * TOP, EXPERTS)
    earlier = (jnp.cumsum(per_source, axis=1) - per_source).astype(jnp.int32)
    position = lax.optimization_barrier(jnp.sum(earlier * per_source, axis=2)).astype(jnp.int32).reshape(-1)
    source = (jnp.arange(count_all, dtype=jnp.int32) // (TOK_DEV * TOP)).astype(jnp.int32)
    slot_index = (source * CAP + position).astype(jnp.int32)
    token_index = (jnp.arange(count_all, dtype=jnp.int32) // TOP).astype(jnp.int32)
    buffer = jnp.zeros((EXPERTS, N_DP * CAP, D), jnp.bfloat16).at[assigned, slot_index].set(upstream[token_index])
    row_grads, combine_grads = lax.map(expert_backward, (buffer, gate_up_w, down_w, saved))
    token_rows = row_grads[assigned, slot_index].reshape(TOKENS, TOP, D).astype(jnp.float32)
    token_combine = combine_grads[assigned, slot_index].reshape(TOKENS, TOP).astype(jnp.float32)
    return router_backward(normed, chosen, router_w, token_rows, token_combine, EXPERTS)

def newton_step(iterate, gram):
    square = jnp.dot(gram, gram, preferred_element_type=jnp.float32)
    poly = (newton_b * gram.astype(jnp.float32) + newton_c * square).astype(jnp.bfloat16)
    product = jnp.dot(iterate, poly, preferred_element_type=jnp.float32)
    return (newton_a * iterate.astype(jnp.float32) + product).astype(jnp.bfloat16)

def muon_section(latent_in, lat_grad, moment_old):
    grad = lax.dot_general(latent_in, lat_grad, (((0,), (0,)), ((), ())), preferred_element_type=jnp.float32)
    moment = momentum_decay * moment_old + grad
    norm_value = jnp.sqrt(jnp.sum(moment * moment))
    iterate = (moment / (norm_value + epsilon)).astype(jnp.bfloat16)
    for sweep in range(NS_ITERS):
        gram = lax.dot_general(iterate, iterate, (((0,), (0,)), ((), ())), preferred_element_type=jnp.float32).astype(jnp.bfloat16)
        iterate = newton_step(iterate, gram)
    update_scale = 0.2 * math.sqrt(max(D, KVA))
    return (moment, (iterate.astype(jnp.float32) * update_scale).astype(jnp.bfloat16))

def reference(normed_input, output_grad, expert_ids, router_weight, gate_up, down_weight, saved_preact, latent_input, latent_grad, momentum):
    section_grads = lax.map(section_backward, (normed_input, output_grad, expert_ids, router_weight, gate_up, down_weight, saved_preact))
    input_grad = jnp.concatenate([section_grads[1:], jnp.zeros_like(section_grads[:1])], axis=0)
    moments = []
    updates = []
    for section_index in range(SECTIONS):
        moment, update = muon_section(latent_input[section_index], latent_grad[section_index], momentum[section_index])
        moments.append(moment)
        updates.append(update)
    return (input_grad, jnp.stack(moments), jnp.stack(updates))
```

```python
import functools
import math

import jax
import jax.numpy as jnp
from jax import lax
from jax.experimental import pallas as pl
from jax.experimental.pallas import tpu as pltpu
from jax.sharding import Mesh, PartitionSpec as P

route_scale = 2.446
momentum_decay = 0.95
newton_a = 3.4445
newton_b = -4.775
newton_c = 2.0315
epsilon = 1e-07

COLUMNS, CORES = 2, 2
PLANE = COLUMNS * CORES
META = 128
HIGHEST = lax.Precision.HIGHEST
F32, BF16 = jnp.float32, jnp.bfloat16
VMEM_LIMIT = 60 * 1024 * 1024


def hop(value, axis, steps):
    count = lax.axis_size(axis)
    return lax.ppermute(value, axis, [(i, (i + steps) % count) for i in range(count)])


def hop_far(value):
    planes = lax.axis_size("z")
    moves = [(p * CORES + c, (p + 1 - 2 * c) % planes * CORES + c) for p in range(planes) for c in range(CORES)]
    return lax.ppermute(value, ("z", "core"), moves)


def call(body, out_shape, in_specs, scratch=(), after=()):
    def apply(*operands):
        skip = len(operands)

        def ordered(*refs):
            body(*refs[:skip], *refs[skip + len(after) :])

        return pl.pallas_call(
            ordered if after else body,
            grid=(1,),
            out_shape=out_shape,
            in_specs=list(in_specs) + [pl.BlockSpec(memory_space=pl.ANY)] * len(after),
            scratch_shapes=scratch,
            compiler_params=pltpu.CompilerParams(vmem_limit_bytes=VMEM_LIMIT),
            cost_estimate=pl.CostEstimate(flops=0, bytes_accessed=0, transcendentals=0),
        )(*operands, *after)

    return apply


def spec():
    return pl.BlockSpec(memory_space=pltpu.VMEM)


def meta_spec(tokens, width):
    return pl.BlockSpec((tokens, META), lambda i: (0, width // META))


SCALAR = pl.BlockSpec(memory_space=pltpu.SMEM)
ANY = pl.BlockSpec(memory_space=pl.ANY)


def flipped(bit, turn):
    return bit + turn - 2 * bit * turn


def plane_lanes(where, experts, capacity, offset):
    lanes = PLANE * capacity
    row = lax.broadcasted_iota(jnp.int32, (META, lanes), 0)
    place = lax.broadcasted_iota(jnp.int32, (META, lanes), 1) // capacity
    column = flipped(where[0], place // CORES)
    core = flipped(where[2], place % CORES)
    expert = column * (experts // COLUMNS) + CORES * where[1] + core
    return (row == expert + offset).astype(BF16)


def slot_map(meta, where, experts, capacity):
    at = jnp.dot(meta, plane_lanes(where, experts, capacity, 0), preferred_element_type=F32)
    slot = lax.broadcasted_iota(jnp.int32, at.shape, 1) % capacity
    return at == slot.astype(F32)


def head_kernel(normed_ref, up_ref, ids_ref, router_ref, pay_ref, picked_ref):
    tokens, width = normed_ref.shape
    experts = router_ref.shape[0]
    logits = lax.dot_general(
        router_ref[...],
        normed_ref[...].astype(F32),
        (((1,), (1,)), ((), ())),
        precision=HIGHEST,
        preferred_element_type=F32,
    )
    scores = jax.nn.sigmoid(logits)
    expert = lax.broadcasted_iota(jnp.int32, (experts, tokens), 0)
    chosen = jnp.zeros((experts, tokens), F32)
    for k in range(ids_ref.shape[0]):
        chosen = chosen + (ids_ref[k : k + 1, :] == expert).astype(F32)
    picked = scores * chosen
    weights = route_scale * picked / jnp.sum(picked, axis=0, keepdims=True)
    before = (
        lax.broadcasted_iota(jnp.int32, (tokens, tokens), 0)
        < lax.broadcasted_iota(jnp.int32, (tokens, tokens), 1)
    ).astype(BF16)
    earlier = jnp.dot(chosen.astype(BF16), before, preferred_element_type=F32)
    position = jnp.where(chosen > 0.5, earlier, -1.0)
    high = weights.astype(BF16).astype(F32)
    meta = jnp.concatenate(
        [position, high, weights - high, jnp.zeros((META - 3 * experts, tokens), F32)], axis=0
    )
    pay_ref[:, :width] = up_ref[...]
    pay_ref[:, width:] = meta.T.astype(BF16)
    picked_ref[...] = picked


def compact_kernel(count, experts, capacity, where, *refs):
    blocks, own_ref, other_ref = refs[:count], refs[count], refs[count + 1]
    width = own_ref.shape[-1]
    for i in range(count):
        block = blocks[i]
        chosen = slot_map(block[:, width:], where, experts, capacity).astype(BF16)
        rows = lax.dot_general(
            chosen, block[:, :width], (((0,), (0,)), ((), ())), preferred_element_type=F32
        ).astype(BF16)
        rows = rows.reshape(COLUMNS, CORES, capacity, width)
        own_ref[:, i] = rows[0]
        other_ref[:, i] = rows[1]


def expert_kernel(groups, capacity, planes, experts, where, *refs):
    count = len(groups)
    rows_refs, refs = refs[: 2 * count], refs[2 * count :]
    saved_refs, down_refs, gate_up_refs, refs = refs[0:2], refs[2:4], refs[4:6], refs[6:]
    own_refs, other_refs, refs = refs[:count], refs[count : 2 * count], refs[2 * count :]
    saved_buf, down_buf, gate_up_buf, sems, weight_sems = refs
    ffw, width = down_refs[0].shape
    copies, weights = [[], []], []
    for m in range(CORES):
        for group in groups:
            for q in range(COLUMNS):
                for step in group:
                    plane = lax.rem(where[1] + step, planes)
                    source = flipped(where[0], q) * planes + plane
                    start = (source * CORES + where[2]) * capacity
                    at = len(copies[m])
                    copies[m].append(
                        pltpu.make_async_copy(
                            saved_refs[m].at[pl.ds(pl.multiple_of(start, capacity), capacity)],
                            saved_buf.at[m, at],
                            sems.at[m, at],
                        )
                    )
        weights.append(
            (
                pltpu.make_async_copy(down_refs[m], down_buf.at[m], weight_sems.at[m, 0]),
                pltpu.make_async_copy(gate_up_refs[m], gate_up_buf.at[m], weight_sems.at[m, 1]),
            )
        )
        for copy in copies[m]:
            copy.start()
        for copy in weights[m]:
            copy.start()
    for m in range(CORES):
        total = len(copies[m]) * capacity
        for copy in copies[m]:
            copy.wait()
        preact = saved_buf[m].reshape(total, 2 * ffw).astype(F32)
        gate_pre, up_pre = preact[:, :ffw], preact[:, ffw:]
        gate_sigmoid = jax.nn.sigmoid(gate_pre)
        activated = gate_pre * gate_sigmoid
        rows = jnp.concatenate([r[m].reshape(-1, width) for r in rows_refs], axis=0)
        weights[m][0].wait()
        hidden_grad = lax.dot_general(
            rows, down_buf[m], (((1,), (1,)), ((), ())), preferred_element_type=F32
        )
        combine = jnp.sum(hidden_grad * (activated * up_pre), axis=1, keepdims=True)
        gate_grad = hidden_grad * up_pre * gate_sigmoid * (1.0 + gate_pre * (1.0 - gate_sigmoid))
        preact_grad = jnp.concatenate([gate_grad, hidden_grad * activated], axis=1).astype(BF16)
        weights[m][1].wait()
        row_grad = lax.dot_general(
            preact_grad, gate_up_buf[m], (((1,), (1,)), ((), ())), preferred_element_type=F32
        ).astype(BF16)
        expert = where[0] * (experts // COLUMNS) + CORES * where[1] + flipped(where[2], m)
        lane = lax.broadcasted_iota(jnp.int32, (total, META), 1)
        marked = jnp.where(lane == expert, combine, 0.0).astype(BF16)
        at = 0
        for group, own_ref, other_ref in zip(groups, own_refs, other_refs):
            for out in (own_ref, other_ref):
                blocks, size = len(group), len(group) * capacity
                out[m, :, :, :width] = row_grad[at : at + size].reshape(blocks, capacity, width)
                out[m, :, :, width:] = marked[at : at + size].reshape(blocks, capacity, META)
                at += size


def combined(meta, own, other, where, experts, capacity):
    width = own.shape[-1] - META
    rows = jnp.concatenate(
        [own.reshape(CORES * capacity, -1), other.reshape(CORES * capacity, -1)], axis=0
    )
    chosen = slot_map(meta, where, experts, capacity)
    sums = 0.0
    for part in (1, 2):
        weight = jnp.dot(
            meta, plane_lanes(where, experts, capacity, part * experts), preferred_element_type=F32
        )
        weight = jnp.where(chosen, weight, 0.0).astype(BF16)
        sums = sums + jnp.dot(weight, rows[:, :width], preferred_element_type=F32)
    marked = jnp.dot(chosen.astype(BF16), rows[:, width:], preferred_element_type=F32)
    return sums, marked


def partial_kernel(experts, capacity, where, *refs):
    count = (len(refs) - 2) // 2
    metas, own_ref, other_ref, outs = refs[:count], refs[count], refs[count + 1], refs[count + 2 :]
    width = own_ref.shape[-1] - META
    for i in range(count):
        sums, marked = combined(
            metas[i][...], own_ref[:, i], other_ref[:, i], where, experts, capacity
        )
        outs[i][:, :width] = sums.astype(outs[i].dtype)
        outs[i][:, width:] = marked.astype(outs[i].dtype)


def last_kernel(own_ref, left_in, right_in, picked_ref, router_ref, out_ref):
    experts, width = router_ref.shape
    moe = own_ref[:, :width] + (left_in[:, :width].astype(F32) + right_in[:, :width].astype(F32))
    token_combine = own_ref[:, width:] + (
        left_in[:, width:].astype(F32) + right_in[:, width:].astype(F32)
    )
    token_combine = token_combine.T[:experts]
    picked = picked_ref[...]
    denominator = jnp.sum(picked, axis=0, keepdims=True)
    select = route_scale * (
        token_combine / denominator
        - jnp.sum(token_combine * picked, axis=0, keepdims=True) / (denominator * denominator)
    )
    logit_grad = select * picked * (1.0 - picked)
    router = lax.dot_general(
        logit_grad,
        router_ref[...],
        (((0,), (0,)), ((), ())),
        precision=HIGHEST,
        preferred_element_type=F32,
    )
    out_ref[...] = (moe + router).astype(BF16)


def grad_kernel(planes, where, input_ref, grad_ref, own_ref, sibling_ref, buffer):
    buffer[...] = lax.dot_general(
        input_ref[...], grad_ref[...], (((0,), (0,)), ((), ())), preferred_element_type=F32
    )
    rows = own_ref.shape[2]
    for m, out in enumerate((own_ref, sibling_ref)):
        core = flipped(where[2], m)
        for q in range(COLUMNS):
            column = flipped(where[0], q)
            for plane in range(planes):
                start = ((column * planes + plane) * CORES + core) * rows
                piece = buffer[pl.ds(pl.multiple_of(start, rows), rows), :]
                out[plane, q] = piece.astype(BF16)


def add_kernel(first_ref, second_ref, out_ref):
    out_ref[...] = (first_ref[...].astype(F32) + second_ref[...].astype(F32)).astype(BF16)


def moment_kernel(kept_ref, other_ref, momentum_ref, moment_ref, rounded_ref):
    moment = momentum_decay * momentum_ref[...] + (
        kept_ref[...].astype(F32) + other_ref[...].astype(F32)
    )
    moment_ref[...] = moment
    rounded_ref[...] = moment.astype(BF16)


def gram_kernel(rows_ref, gram_ref):
    rows = rows_ref[...]
    gram_ref[...] = lax.dot_general(
        rows, rows, (((0,), (0,)), ((), ())), preferred_element_type=F32
    )


def polynomial(gram):
    square = jnp.dot(gram, gram, preferred_element_type=F32)
    return (newton_b * gram.astype(F32) + newton_c * square).astype(BF16)


def advance(iterate, poly):
    product = jnp.dot(iterate, poly, preferred_element_type=F32)
    return (newton_a * iterate.astype(F32) + product).astype(BF16)


def newton_kernel(update_scale, own_ref, other_ref, moment_ref, update_ref):
    gram = own_ref[...] + other_ref[...]
    size = gram.shape[0]
    diagonal = lax.broadcasted_iota(jnp.int32, (size, size), 0) == lax.broadcasted_iota(
        jnp.int32, (size, size), 1
    )
    squares = jnp.sum(jnp.where(diagonal, gram, 0.0), axis=0, keepdims=True)
    inverse = 1.0 / (jnp.sqrt(jnp.sum(squares, axis=1, keepdims=True)) + epsilon)
    gram = gram * inverse * inverse
    iterate = (moment_ref[...] * inverse).astype(BF16)
    rounded = gram.astype(BF16)
    poly = polynomial(rounded)
    mixed = jnp.dot(rounded, poly, preferred_element_type=F32)
    bent = jnp.dot(poly, mixed.astype(BF16), preferred_element_type=F32)
    next_gram = newton_a * newton_a * gram + 2.0 * newton_a * mixed + bent
    iterate = advance(iterate, poly)
    iterate = advance(iterate, polynomial(next_gram.astype(BF16)))
    update_ref[...] = (iterate.astype(F32) * update_scale).astype(BF16)


def on_device(
    normed_input,
    output_grad,
    expert_ids,
    router_weight,
    gate_up,
    down_weight,
    saved_preact,
    latent_input,
    latent_grad,
    momentum,
):
    normed, upstream, chosen = normed_input[0], output_grad[0], expert_ids[0]
    router_w, gate_up_w, down_w = router_weight[0], gate_up[0, 0], down_weight[0, 0]
    saved = saved_preact[0, 0]
    tokens, width = normed.shape
    experts = router_w.shape[1]
    planes = lax.axis_size("z")
    capacity = saved.shape[0] // (PLANE * planes)
    yh, z, core = lax.axis_index("yh"), lax.axis_index("z"), lax.axis_index("core")
    where = jnp.stack([yh, z, core]).astype(jnp.int32)
    wide = width + META
    ffw = down_w.shape[0]

    def shape(*dims, dtype=BF16):
        return jax.ShapeDtypeStruct(dims, dtype)

    def compact(*blocks, after=()):
        count = len(blocks)
        return call(
            functools.partial(compact_kernel, count, experts, capacity),
            (shape(CORES, count, capacity, width),) * 2,
            [SCALAR] + [spec()] * count,
            after=after,
        )(where, *blocks)

    def backward(groups, rows, after=()):
        blocks = COLUMNS * sum(len(group) for group in groups)
        outs = call(
            functools.partial(expert_kernel, groups, capacity, planes, experts),
            tuple(shape(CORES, len(group), capacity, wide) for group in groups) * 2,
            [SCALAR] + [spec()] * (2 * len(groups)) + [ANY] * 6,
            scratch=[
                pltpu.VMEM((CORES, blocks, capacity, 2 * ffw), BF16),
                pltpu.VMEM((CORES,) + down_w.shape, BF16),
                pltpu.VMEM((CORES,) + gate_up_w.shape, BF16),
                pltpu.SemaphoreType.DMA((CORES, blocks)),
                pltpu.SemaphoreType.DMA((CORES, 2)),
            ],
            after=after,
        )(where, *[part for pair in rows for part in pair], *both_saved, *both_down, *both_gate_up)
        return outs[: len(groups)], outs[len(groups) :]

    def partial(blocks, own, other, dtype, after=()):
        return call(
            functools.partial(partial_kernel, experts, capacity),
            (shape(tokens, wide, dtype=dtype),) * len(blocks),
            [SCALAR] + [meta_spec(tokens, width)] * len(blocks) + [spec()] * 2,
            after=after,
        )(where, *blocks, own, other)

    sync = lax.optimization_barrier

    def to_other(rows):
        return hop(rows, "yh", 1)

    def around(up, down):
        return hop(up, "z", 1), hop(down, "z", -1)

    own_rows, columns = momentum.shape[1], momentum.shape[2]
    last = planes // 2

    router_t = router_w.T
    pay, picked = call(
        head_kernel,
        (shape(tokens, wide), shape(experts, tokens, dtype=F32)),
        [spec()] * 4,
    )(normed, upstream, chosen.T, router_t)

    up, down = around(pay, pay)
    own0, other0 = compact(pay)
    other0 = to_other(other0)
    both_saved = (saved, hop(saved, "core", 1))
    both_down = (down_w, hop(down_w, "core", 1))
    both_gate_up = (gate_up_w, hop(gate_up_w, "core", 1))
    up, down, other0 = sync((up, down, other0))
    ups, downs = [pay, up], [pay, down]

    up, down = around(up, down)
    own1, other1 = compact(ups[1], downs[1])
    other1 = to_other(other1)
    piece = shape(planes, COLUMNS, own_rows, columns)
    grad_kept, grad_given = call(
        functools.partial(grad_kernel, planes),
        (piece, piece),
        [SCALAR, spec(), spec()],
        scratch=[pltpu.VMEM((width, columns), F32)],
        after=[own1],
    )(where, latent_input[0], latent_grad[0])
    up, down, other1, grad_kept, grad_given = sync((up, down, other1, grad_kept, grad_given))
    ups.append(up)
    downs.append(down)

    up, down = around(up, down)
    own2, other2 = compact(ups[2], downs[2])
    other2 = to_other(other2)
    summed = call(add_kernel, piece, [spec()] * 2, after=[own2])(
        grad_kept, hop(grad_given, "core", 1)
    )
    up, down, own2 = sync((up, down, own2))
    ups.append(up)
    downs.append(down)

    far = hop_far(jnp.where(core == 0, up, down))
    own3, other3 = compact(ups[3], downs[3], after=[summed])
    other3 = to_other(other3)
    grad_rows = lax.psum_scatter(summed, "z", scatter_dimension=0, tiled=True)
    (done0, done1), (given0, given1) = backward(
        [[0], [planes - 1, 1]], [(own0, other0), (own1, other1)], after=[own3]
    )
    far, other2, done1, given0, given1 = sync((far, other2, done1, given0, given1))
    given1 = to_other(given1)

    own4, other4 = compact(far)
    other4 = to_other(other4)
    (done2, done3), (given2, given3) = backward(
        [[planes - 2, 2], [planes - 3, 3]], [(own2, other2), (own3, other3)], after=[own4]
    )
    other4, done2, done3, given1, given2, given3, grad_rows = sync(
        (other4, done2, done3, given1, given2, given3, grad_rows)
    )
    given3 = to_other(given3)
    (done4,), (given4,) = backward([[last]], [(own4, other4)])
    given4 = to_other(given4)
    moment, rounded = call(
        moment_kernel,
        (shape(own_rows, columns, dtype=F32), shape(own_rows, columns)),
        [spec()] * 3,
        after=[done4],
    )(grad_rows[0, 0], to_other(grad_rows[0, 1]), momentum[0])
    rounded_other = to_other(rounded)
    given4, given3, given2, rounded_other = sync((given4, given3, given2, rounded_other))
    rounded = jnp.concatenate([rounded, rounded_other], axis=0)
    rounded = lax.all_gather(rounded, "z", axis=0, tiled=True)
    given2 = to_other(given2)

    (total,) = partial([far], done4, given4, BF16)
    total = hop_far(total)
    to_low, to_high = partial([ups[3], downs[3]], done3, given3, F32)
    total, to_low, to_high, given0 = sync((total, to_low, to_high, given0))
    given0 = to_other(given0)
    total = total.astype(F32)
    up = (to_high + jnp.where(core == 0, total, 0.0)).astype(BF16)
    down = (to_low + jnp.where(core == 0, 0.0, total)).astype(BF16)

    up, down = around(up, down)
    to_low, to_high = partial([ups[2], downs[2]], done2, given2, F32)
    up, down, to_low, to_high, given0, rounded = sync(
        (up, down, to_low, to_high, given0, rounded)
    )
    up, down = (to_high + up.astype(F32)).astype(BF16), (to_low + down.astype(F32)).astype(BF16)

    up, down = around(up, down)
    to_low, to_high = partial([ups[1], downs[1]], done1, given1, F32)
    gram = call(
        gram_kernel, shape(columns, columns, dtype=F32), [spec()], after=[to_low]
    )(rounded)
    up, down, to_low, to_high, gram = sync((up, down, to_low, to_high, gram))
    up, down = (to_high + up.astype(F32)).astype(BF16), (to_low + down.astype(F32)).astype(BF16)

    up, down = around(up, down)
    (home,) = partial([pay], done0, given0, F32)
    update = call(
        functools.partial(newton_kernel, 0.2 * math.sqrt(max(width, columns))),
        shape(own_rows, columns),
        [spec()] * 3,
        after=[home],
    )(gram, hop(gram, "core", 1), moment)
    up, down, home, update = sync((up, down, home, update))
    section_grad = call(last_kernel, shape(tokens, width), [spec()] * 5)(
        home, down, up, picked, router_t
    )
    sections = lax.axis_size("section")
    passed = lax.ppermute(section_grad, "section", [(s, s - 1) for s in range(1, sections)])
    return (passed[None], moment[None], update[None])


def solution(mesh):
    sections, group = mesh.shape["section"], mesh.shape["dp"]
    fine = Mesh(
        mesh.devices.reshape(sections, COLUMNS, group // PLANE, CORES),
        ("section", "yh", "z", "core"),
    )
    dp = ("yh", "z", "core")
    split = P("section", dp)
    return jax.shard_map(
        on_device,
        mesh=fine,
        in_specs=(split, split, split, P("section"), split, split, split, split, split, split),
        out_specs=(split, split, split),
        check_vma=False,
    )
```

```python
import functools
import math

import jax
import jax.numpy as jnp
from jax import lax
from jax.experimental import pallas as pl
from jax.experimental.pallas import tpu as pltpu
from jax.sharding import Mesh, PartitionSpec as P

route_scale = 2.446
momentum_decay = 0.95
newton_a = 3.4445
newton_b = -4.775
newton_c = 2.0315
epsilon = 1e-07

COLUMNS, CORES = 2, 2
PLANE = COLUMNS * CORES
META = 128
HIGHEST = lax.Precision.HIGHEST
F32, BF16 = jnp.float32, jnp.bfloat16
VMEM_LIMIT = 60 * 1024 * 1024


def hop(value, axis, steps):
    count = lax.axis_size(axis)
    return lax.ppermute(value, axis, [(i, (i + steps) % count) for i in range(count)])


def hop_far(value):
    planes = lax.axis_size("z")
    moves = [(p * CORES + c, (p + 1 - 2 * c) % planes * CORES + c) for p in range(planes) for c in range(CORES)]
    return lax.ppermute(value, ("z", "core"), moves)


def call(body, out_shape, in_specs, scratch=(), after=()):
    def apply(*operands):
        skip = len(operands)

        def ordered(*refs):
            body(*refs[:skip], *refs[skip + len(after) :])

        return pl.pallas_call(
            ordered if after else body,
            grid=(1,),
            out_shape=out_shape,
            in_specs=list(in_specs) + [pl.BlockSpec(memory_space=pl.ANY)] * len(after),
            scratch_shapes=scratch,
            compiler_params=pltpu.CompilerParams(vmem_limit_bytes=VMEM_LIMIT),
            cost_estimate=pl.CostEstimate(flops=0, bytes_accessed=0, transcendentals=0),
        )(*operands, *after)

    return apply


def spec():
    return pl.BlockSpec(memory_space=pltpu.VMEM)


def meta_spec(tokens, width):
    return pl.BlockSpec((tokens, META), lambda i: (0, width // META))


SCALAR = pl.BlockSpec(memory_space=pltpu.SMEM)
ANY = pl.BlockSpec(memory_space=pl.ANY)


def flipped(bit, turn):
    return bit + turn - 2 * bit * turn


def plane_lanes(where, experts, capacity, offset):
    lanes = PLANE * capacity
    row = lax.broadcasted_iota(jnp.int32, (META, lanes), 0)
    place = lax.broadcasted_iota(jnp.int32, (META, lanes), 1) // capacity
    column = flipped(where[0], place // CORES)
    core = flipped(where[2], place % CORES)
    expert = column * (experts // COLUMNS) + CORES * where[1] + core
    return (row == expert + offset).astype(BF16)


def slot_map(meta, where, experts, capacity):
    at = jnp.dot(meta, plane_lanes(where, experts, capacity, 0), preferred_element_type=F32)
    slot = lax.broadcasted_iota(jnp.int32, at.shape, 1) % capacity
    return at == slot.astype(F32)


def head_kernel(normed_ref, up_ref, ids_ref, router_ref, pay_ref, picked_ref):
    tokens, width = normed_ref.shape
    experts = router_ref.shape[0]
    logits = lax.dot_general(
        router_ref[...],
        normed_ref[...].astype(F32),
        (((1,), (1,)), ((), ())),
        precision=HIGHEST,
        preferred_element_type=F32,
    )
    scores = jax.nn.sigmoid(logits)
    expert = lax.broadcasted_iota(jnp.int32, (experts, tokens), 0)
    chosen = jnp.zeros((experts, tokens), F32)
    for k in range(ids_ref.shape[0]):
        chosen = chosen + (ids_ref[k : k + 1, :] == expert).astype(F32)
    picked = scores * chosen
    weights = route_scale * picked / jnp.sum(picked, axis=0, keepdims=True)
    before = (
        lax.broadcasted_iota(jnp.int32, (tokens, tokens), 0)
        < lax.broadcasted_iota(jnp.int32, (tokens, tokens), 1)
    ).astype(BF16)
    earlier = jnp.dot(chosen.astype(BF16), before, preferred_element_type=F32)
    position = jnp.where(chosen > 0.5, earlier, -1.0)
    high = weights.astype(BF16).astype(F32)
    meta = jnp.concatenate(
        [position, high, weights - high, jnp.zeros((META - 3 * experts, tokens), F32)], axis=0
    )
    pay_ref[:, :width] = up_ref[...]
    pay_ref[:, width:] = meta.T.astype(BF16)
    picked_ref[...] = picked


def compact_kernel(count, experts, capacity, where, *refs):
    blocks, own_ref, other_ref = refs[:count], refs[count], refs[count + 1]
    width = own_ref.shape[-1]
    for i in range(count):
        block = blocks[i]
        chosen = slot_map(block[:, width:], where, experts, capacity).astype(BF16)
        rows = lax.dot_general(
            chosen, block[:, :width], (((0,), (0,)), ((), ())), preferred_element_type=F32
        ).astype(BF16)
        rows = rows.reshape(COLUMNS, CORES, capacity, width)
        own_ref[:, i] = rows[0]
        other_ref[:, i] = rows[1]


def expert_kernel(groups, capacity, planes, experts, where, *refs):
    count = len(groups)
    rows_refs, refs = refs[: 2 * count], refs[2 * count :]
    saved_refs, down_refs, gate_up_refs, refs = refs[0:2], refs[2:4], refs[4:6], refs[6:]
    own_refs, other_refs, refs = refs[:count], refs[count : 2 * count], refs[2 * count :]
    saved_buf, down_buf, gate_up_buf, sems, weight_sems = refs
    ffw, width = down_refs[0].shape
    copies, weights = [[], []], []
    for m in range(CORES):
        for group in groups:
            for q in range(COLUMNS):
                for step in group:
                    plane = lax.rem(where[1] + step, planes)
                    source = flipped(where[0], q) * planes + plane
                    start = (source * CORES + where[2]) * capacity
                    at = len(copies[m])
                    copies[m].append(
                        pltpu.make_async_copy(
                            saved_refs[m].at[pl.ds(pl.multiple_of(start, capacity), capacity)],
                            saved_buf.at[m, at],
                            sems.at[m, at],
                        )
                    )
        weights.append(
            (
                pltpu.make_async_copy(down_refs[m], down_buf.at[m], weight_sems.at[m, 0]),
                pltpu.make_async_copy(gate_up_refs[m], gate_up_buf.at[m], weight_sems.at[m, 1]),
            )
        )
        for copy in copies[m]:
            copy.start()
        for copy in weights[m]:
            copy.start()
    for m in range(CORES):
        total = len(copies[m]) * capacity
        for copy in copies[m]:
            copy.wait()
        preact = saved_buf[m].reshape(total, 2 * ffw).astype(F32)
        gate_pre, up_pre = preact[:, :ffw], preact[:, ffw:]
        gate_sigmoid = jax.nn.sigmoid(gate_pre)
        activated = gate_pre * gate_sigmoid
        rows = jnp.concatenate([r[m].reshape(-1, width) for r in rows_refs], axis=0)
        weights[m][0].wait()
        hidden_grad = lax.dot_general(
            rows, down_buf[m], (((1,), (1,)), ((), ())), preferred_element_type=F32
        )
        combine = jnp.sum(hidden_grad * (activated * up_pre), axis=1, keepdims=True)
        gate_grad = hidden_grad * up_pre * gate_sigmoid * (1.0 + gate_pre * (1.0 - gate_sigmoid))
        preact_grad = jnp.concatenate([gate_grad, hidden_grad * activated], axis=1).astype(BF16)
        weights[m][1].wait()
        row_grad = lax.dot_general(
            preact_grad, gate_up_buf[m], (((1,), (1,)), ((), ())), preferred_element_type=F32
        ).astype(BF16)
        expert = where[0] * (experts // COLUMNS) + CORES * where[1] + flipped(where[2], m)
        lane = lax.broadcasted_iota(jnp.int32, (total, META), 1)
        marked = jnp.where(lane == expert, combine, 0.0).astype(BF16)
        at = 0
        for group, own_ref, other_ref in zip(groups, own_refs, other_refs):
            for out in (own_ref, other_ref):
                blocks, size = len(group), len(group) * capacity
                out[m, :, :, :width] = row_grad[at : at + size].reshape(blocks, capacity, width)
                out[m, :, :, width:] = marked[at : at + size].reshape(blocks, capacity, META)
                at += size


def combined(meta, own, other, where, experts, capacity):
    width = own.shape[-1] - META
    rows = jnp.concatenate(
        [own.reshape(CORES * capacity, -1), other.reshape(CORES * capacity, -1)], axis=0
    )
    chosen = slot_map(meta, where, experts, capacity)
    sums = 0.0
    for part in (1, 2):
        weight = jnp.dot(
            meta, plane_lanes(where, experts, capacity, part * experts), preferred_element_type=F32
        )
        weight = jnp.where(chosen, weight, 0.0).astype(BF16)
        sums = sums + jnp.dot(weight, rows[:, :width], preferred_element_type=F32)
    marked = jnp.dot(chosen.astype(BF16), rows[:, width:], preferred_element_type=F32)
    return sums, marked


def partial_kernel(experts, capacity, where, *refs):
    count = (len(refs) - 2) // 2
    metas, own_ref, other_ref, outs = refs[:count], refs[count], refs[count + 1], refs[count + 2 :]
    width = own_ref.shape[-1] - META
    for i in range(count):
        sums, marked = combined(
            metas[i][...], own_ref[:, i], other_ref[:, i], where, experts, capacity
        )
        outs[i][:, :width] = sums.astype(outs[i].dtype)
        outs[i][:, width:] = marked.astype(outs[i].dtype)


def last_kernel(own_ref, left_in, right_in, picked_ref, router_ref, out_ref):
    experts, width = router_ref.shape
    moe = own_ref[:, :width] + (left_in[:, :width].astype(F32) + right_in[:, :width].astype(F32))
    token_combine = own_ref[:, width:] + (
        left_in[:, width:].astype(F32) + right_in[:, width:].astype(F32)
    )
    token_combine = token_combine.T[:experts]
    picked = picked_ref[...]
    denominator = jnp.sum(picked, axis=0, keepdims=True)
    select = route_scale * (
        token_combine / denominator
        - jnp.sum(token_combine * picked, axis=0, keepdims=True) / (denominator * denominator)
    )
    logit_grad = select * picked * (1.0 - picked)
    router = lax.dot_general(
        logit_grad,
        router_ref[...],
        (((0,), (0,)), ((), ())),
        precision=HIGHEST,
        preferred_element_type=F32,
    )
    out_ref[...] = (moe + router).astype(BF16)


def grad_kernel(planes, where, input_ref, grad_ref, own_ref, sibling_ref, buffer):
    buffer[...] = lax.dot_general(
        input_ref[...], grad_ref[...], (((0,), (0,)), ((), ())), preferred_element_type=F32
    )
    rows = own_ref.shape[2]
    for m, out in enumerate((own_ref, sibling_ref)):
        core = flipped(where[2], m)
        for q in range(COLUMNS):
            column = flipped(where[0], q)
            for plane in range(planes):
                start = ((column * planes + plane) * CORES + core) * rows
                piece = buffer[pl.ds(pl.multiple_of(start, rows), rows), :]
                out[plane, q] = piece.astype(BF16)


def add_kernel(first_ref, second_ref, out_ref):
    out_ref[...] = (first_ref[...].astype(F32) + second_ref[...].astype(F32)).astype(BF16)


def moment_kernel(kept_ref, other_ref, momentum_ref, moment_ref, rounded_ref):
    moment = momentum_decay * momentum_ref[...] + (
        kept_ref[...].astype(F32) + other_ref[...].astype(F32)
    )
    moment_ref[...] = moment
    rounded_ref[...] = moment.astype(BF16)


def gram_kernel(rows_ref, gram_ref):
    rows = rows_ref[...]
    gram_ref[...] = lax.dot_general(
        rows, rows, (((0,), (0,)), ((), ())), preferred_element_type=F32
    )


def polynomial(gram):
    square = jnp.dot(gram, gram, preferred_element_type=F32)
    return (newton_b * gram.astype(F32) + newton_c * square).astype(BF16)


def advance(iterate, poly):
    product = jnp.dot(iterate, poly, preferred_element_type=F32)
    return (newton_a * iterate.astype(F32) + product).astype(BF16)


def newton_kernel(update_scale, own_ref, other_ref, moment_ref, update_ref):
    gram = own_ref[...] + other_ref[...]
    size = gram.shape[0]
    diagonal = lax.broadcasted_iota(jnp.int32, (size, size), 0) == lax.broadcasted_iota(
        jnp.int32, (size, size), 1
    )
    squares = jnp.sum(jnp.where(diagonal, gram, 0.0), axis=0, keepdims=True)
    inverse = 1.0 / (jnp.sqrt(jnp.sum(squares, axis=1, keepdims=True)) + epsilon)
    gram = gram * inverse * inverse
    iterate = (moment_ref[...] * inverse).astype(BF16)
    rounded = gram.astype(BF16)
    poly = polynomial(rounded)
    mixed = jnp.dot(rounded, poly, preferred_element_type=F32)
    bent = jnp.dot(poly, mixed.astype(BF16), preferred_element_type=F32)
    next_gram = newton_a * newton_a * gram + 2.0 * newton_a * mixed + bent
    iterate = advance(iterate, poly)
    iterate = advance(iterate, polynomial(next_gram.astype(BF16)))
    update_ref[...] = (iterate.astype(F32) * update_scale).astype(BF16)


def on_device(
    normed_input,
    output_grad,
    expert_ids,
    router_weight,
    gate_up,
    down_weight,
    saved_preact,
    latent_input,
    latent_grad,
    momentum,
):
    normed, upstream, chosen = normed_input[0], output_grad[0], expert_ids[0]
    router_w, gate_up_w, down_w = router_weight[0], gate_up[0, 0], down_weight[0, 0]
    saved = saved_preact[0, 0]
    tokens, width = normed.shape
    experts = router_w.shape[1]
    planes = lax.axis_size("z")
    capacity = saved.shape[0] // (PLANE * planes)
    yh, z, core = lax.axis_index("yh"), lax.axis_index("z"), lax.axis_index("core")
    where = jnp.stack([yh, z, core]).astype(jnp.int32)
    wide = width + META
    ffw = down_w.shape[0]

    def shape(*dims, dtype=BF16):
        return jax.ShapeDtypeStruct(dims, dtype)

    def compact(*blocks, after=()):
        count = len(blocks)
        return call(
            functools.partial(compact_kernel, count, experts, capacity),
            (shape(CORES, count, capacity, width),) * 2,
            [SCALAR] + [spec()] * count,
            after=after,
        )(where, *blocks)

    def backward(groups, rows, after=()):
        blocks = COLUMNS * sum(len(group) for group in groups)
        outs = call(
            functools.partial(expert_kernel, groups, capacity, planes, experts),
            tuple(shape(CORES, len(group), capacity, wide) for group in groups) * 2,
            [SCALAR] + [spec()] * (2 * len(groups)) + [ANY] * 6,
            scratch=[
                pltpu.VMEM((CORES, blocks, capacity, 2 * ffw), BF16),
                pltpu.VMEM((CORES,) + down_w.shape, BF16),
                pltpu.VMEM((CORES,) + gate_up_w.shape, BF16),
                pltpu.SemaphoreType.DMA((CORES, blocks)),
                pltpu.SemaphoreType.DMA((CORES, 2)),
            ],
            after=after,
        )(where, *[part for pair in rows for part in pair], *both_saved, *both_down, *both_gate_up)
        return outs[: len(groups)], outs[len(groups) :]

    def partial(blocks, own, other, dtype, after=()):
        return call(
            functools.partial(partial_kernel, experts, capacity),
            (shape(tokens, wide, dtype=dtype),) * len(blocks),
            [SCALAR] + [meta_spec(tokens, width)] * len(blocks) + [spec()] * 2,
            after=after,
        )(where, *blocks, own, other)

    sync = lax.optimization_barrier

    def to_other(rows):
        return hop(rows, "yh", 1)

    def around(up, down):
        return hop(up, "z", 1), hop(down, "z", -1)

    own_rows, columns = momentum.shape[1], momentum.shape[2]
    last = planes // 2

    router_t = router_w.T
    pay, picked = call(
        head_kernel,
        (shape(tokens, wide), shape(experts, tokens, dtype=F32)),
        [spec()] * 4,
    )(normed, upstream, chosen.T, router_t)

    up, down = around(pay, pay)
    own0, other0 = compact(pay)
    other0 = to_other(other0)
    both_saved = (saved, hop(saved, "core", 1))
    both_down = (down_w, hop(down_w, "core", 1))
    both_gate_up = (gate_up_w, hop(gate_up_w, "core", 1))
    up, down, other0 = sync((up, down, other0))
    ups, downs = [pay, up], [pay, down]

    up, down = around(up, down)
    own1, other1 = compact(ups[1], downs[1])
    other1 = to_other(other1)
    piece = shape(planes, COLUMNS, own_rows, columns)
    grad_kept, grad_given = call(
        functools.partial(grad_kernel, planes),
        (piece, piece),
        [SCALAR, spec(), spec()],
        scratch=[pltpu.VMEM((width, columns), F32)],
        after=[own1],
    )(where, latent_input[0], latent_grad[0])
    up, down, other1, grad_kept, grad_given = sync((up, down, other1, grad_kept, grad_given))
    ups.append(up)
    downs.append(down)

    up, down = around(up, down)
    own2, other2 = compact(ups[2], downs[2])
    other2 = to_other(other2)
    summed = call(add_kernel, piece, [spec()] * 2, after=[own2])(
        grad_kept, hop(grad_given, "core", 1)
    )
    up, down, own2 = sync((up, down, own2))
    ups.append(up)
    downs.append(down)

    far = hop_far(jnp.where(core == 0, up, down))
    own3, other3 = compact(ups[3], downs[3], after=[summed])
    other3 = to_other(other3)
    grad_rows = lax.psum_scatter(summed, "z", scatter_dimension=0, tiled=True)
    (done0, done1), (given0, given1) = backward(
        [[0], [planes - 1, 1]], [(own0, other0), (own1, other1)], after=[own3]
    )
    far, other2, other3, done1, given0, given1 = sync(
        (far, other2, other3, done1, given0, given1)
    )
    given1 = to_other(given1)

    own4, other4 = compact(far)
    other4 = to_other(other4)
    (done2, done3), (given2, given3) = backward(
        [[planes - 2, 2], [planes - 3, 3]], [(own2, other2), (own3, other3)], after=[own4]
    )
    other4, done2, done3, given1, given2, given3, grad_rows = sync(
        (other4, done2, done3, given1, given2, given3, grad_rows)
    )
    given3 = to_other(given3)
    (done4,), (given4,) = backward([[last]], [(own4, other4)])
    given4 = to_other(given4)
    moment, rounded = call(
        moment_kernel,
        (shape(own_rows, columns, dtype=F32), shape(own_rows, columns)),
        [spec()] * 3,
        after=[done4],
    )(grad_rows[0, 0], to_other(grad_rows[0, 1]), momentum[0])
    rounded_other = to_other(rounded)
    given4, given3, given2, rounded_other = sync((given4, given3, given2, rounded_other))
    rounded = jnp.concatenate([rounded, rounded_other], axis=0)
    rounded = lax.all_gather(rounded, "z", axis=0, tiled=True)
    given2 = to_other(given2)

    (total,) = partial([far], done4, given4, BF16)
    total = hop_far(total)
    to_low, to_high = partial([ups[3], downs[3]], done3, given3, F32)
    total, to_low, to_high, given0 = sync((total, to_low, to_high, given0))
    given0 = to_other(given0)
    total = total.astype(F32)
    up = (to_high + jnp.where(core == 0, total, 0.0)).astype(BF16)
    down = (to_low + jnp.where(core == 0, 0.0, total)).astype(BF16)

    up, down = around(up, down)
    to_low, to_high = partial([ups[2], downs[2]], done2, given2, F32)
    up, down, to_low, to_high, given0, rounded = sync(
        (up, down, to_low, to_high, given0, rounded)
    )
    up, down = (to_high + up.astype(F32)).astype(BF16), (to_low + down.astype(F32)).astype(BF16)

    up, down = around(up, down)
    to_low, to_high = partial([ups[1], downs[1]], done1, given1, F32)
    gram = call(
        gram_kernel, shape(columns, columns, dtype=F32), [spec()], after=[to_low]
    )(rounded)
    up, down, to_low, to_high, gram = sync((up, down, to_low, to_high, gram))
    up, down = (to_high + up.astype(F32)).astype(BF16), (to_low + down.astype(F32)).astype(BF16)

    up, down = around(up, down)
    (home,) = partial([pay], done0, given0, F32)
    update = call(
        functools.partial(newton_kernel, 0.2 * math.sqrt(max(width, columns))),
        shape(own_rows, columns),
        [spec()] * 3,
        after=[home],
    )(gram, hop(gram, "core", 1), moment)
    up, down, home, update = sync((up, down, home, update))
    section_grad = call(last_kernel, shape(tokens, width), [spec()] * 5)(
        home, down, up, picked, router_t
    )
    sections = lax.axis_size("section")
    passed = lax.ppermute(section_grad, "section", [(s, s - 1) for s in range(1, sections)])
    return (passed[None], moment[None], update[None])


def solution(mesh):
    sections, group = mesh.shape["section"], mesh.shape["dp"]
    fine = Mesh(
        mesh.devices.reshape(sections, COLUMNS, group // PLANE, CORES),
        ("section", "yh", "z", "core"),
    )
    dp = ("yh", "z", "core")
    split = P("section", dp)
    return jax.shard_map(
        on_device,
        mesh=fine,
        in_specs=(split, split, split, P("section"), split, split, split, split, split, split),
        out_specs=(split, split, split),
        check_vma=False,
    )
```
